32 devices in a mesh: row: 8 (over y, x, core), col: 4 (over z).
Axes of the slice: x: 2, y: 2, z: 4, core: 2. Of those that a mesh axis runs over, the one named last changes fastest.
Arguments:
- item_factors: bfloat16 [4096, 128], P(('row', 'col')), may hold values from -0.5 to 0.5
- item_index: int32 [256, 2048], P('col', 'row'), may hold values from 0 to 511
- ratings: bfloat16 [256, 2048], P('col', 'row'), may hold values from -4 to 4
- counts: int32 [256, 8], P('col', 'row'), may hold values from 1 to 256, as said below
Outputs:
- user_factors: float32 [4, 64, 128], P('col', 'row')
The draws below stay inside these ranges and needn't reach their ends.
Inputs may be any that keep to these rules, and one draw needn't show every extreme that they name: `counts`: for each user block and item block, some user has exactly 256 live slots.
All inputs are finite; a program needn't handle non-finite values.
Results may differ from the reference program's by a relative error of at most 0.0004.
Values may be sent and summed in bfloat16 or wider, within the bound.
A program may use at most 192 MiB of HBM per device.

```python
import jax
import jax.numpy as jnp
from jax import lax

RANK = 128
SLOTS = 256
ITEM_DEV = 128
USERS = 256
ITEMS = 4096
N_ROW = 8
N_COL = 4


def draw_counts(key, part):
    first, second, third, fourth = jax.random.split(jax.random.fold_in(key, 11), 4)
    tile = jnp.arange(N_ROW, dtype=jnp.int32)
    ceiling = SLOTS // 4 + 3 * SLOTS // 4 * tile // max(N_ROW - 1, 1)
    level = jax.random.randint(fourth, (USERS, 1), 0, 8)
    shift_by = jnp.where(level < 5, 0, 2 * (level - 4)).astype(jnp.int32)
    reach = jnp.maximum(jnp.right_shift(ceiling[None, :], shift_by), 1)
    raw_bits = jax.random.randint(first, (USERS, N_ROW), 0, 1 << 20)
    value = 1 + raw_bits % reach
    heavy = jax.random.randint(second, (USERS, 1), 1, 3)
    value = jnp.minimum(value * heavy, SLOTS)
    user_block = USERS // N_COL
    picked = jax.random.randint(third, (N_COL, N_ROW), 0, user_block)
    within = jnp.arange(USERS, dtype=jnp.int32) % user_block
    block_id = jnp.arange(USERS, dtype=jnp.int32) // user_block
    forced = within[:, None] == picked[block_id]
    return jnp.where(forced, SLOTS, value).astype(jnp.int32)


def set_ends(entries, rng, least, top_value):
    dims = entries.shape
    index_at = [jax.random.randint(jax.random.fold_in(rng, axis), (), 0, dims[axis]) for axis in range(len(dims))]
    entries = entries.at[tuple(index_at)].set(least)
    longest = dims.index(max(dims))
    index_at[longest] = (index_at[longest] + 1) % dims[longest]
    return entries.at[tuple(index_at)].set(top_value)


def block_scale(stream_key, dims, cuts, least, high):
    factor_of, own = 1.0, jax.random.fold_in(stream_key, 6)
    for dim, parts in cuts:
        draws = jnp.exp(jax.random.uniform(jax.random.fold_in(own, dim), (parts,), jnp.float32, least / len(cuts), high / len(cuts)))
        factor_of = factor_of * jnp.repeat(draws, dims[dim] // parts).reshape([-1 if axis == dim else 1 for axis in range(len(dims))])
    return factor_of


def scatter_about(rng, dims, width, limit, pieces=(), kind=jnp.bfloat16):
    values = width * jax.random.normal(rng, dims, jnp.float32)
    if pieces:
        values = values * block_scale(rng, dims, pieces, -0.22, 0.18)
    return jnp.clip(values, -limit, limit).astype(kind)


def setup_inputs(seed: int = 0) -> dict:
    streams_of = jax.random.split(jax.random.key(seed), 5)
    item_factors = scatter_about(streams_of[0], (ITEMS, RANK), RANK ** -0.5, 0.5, ((0, 32),))
    item_index = set_ends(jax.random.randint(streams_of[1], (USERS, N_ROW * SLOTS), 0, N_COL * ITEM_DEV), jax.random.fold_in(streams_of[1], 1), 0, (N_COL * ITEM_DEV) - 1).astype(jnp.int32)
    ratings = scatter_about(streams_of[2], (USERS, N_ROW * SLOTS), 1.0, 4.0, ((0, 4), (1, 8)))
    counts = draw_counts(jax.random.fold_in(streams_of[4], 71), 0)
    return dict(item_factors=item_factors, item_index=item_index, ratings=ratings, counts=counts)


def solve_users(normal_sum, right_side, number):
    width_rank = normal_sum.shape[-1]
    shifted = normal_sum + (0.1 * number / width_rank)[:, None, None] * jnp.eye(width_rank, dtype=jnp.float32)
    factor_low = jnp.linalg.cholesky(shifted)
    middle = jax.scipy.linalg.solve_triangular(factor_low, right_side[:, :, None], lower=True)
    answer = jax.scipy.linalg.solve_triangular(factor_low, middle, lower=True, trans=1)
    return answer[:, :, 0]

def reference(item_factors, item_index, ratings, counts):
    tile_width = N_COL * ITEM_DEV
    slot_tile = jnp.arange(N_ROW * SLOTS, dtype=jnp.int32) // SLOTS
    slot_place = jnp.arange(N_ROW * SLOTS, dtype=jnp.int32) % SLOTS
    global_index = (item_index + (slot_tile * tile_width)[None, :]).astype(jnp.int32)
    live_slot = (slot_place[None, :] < jnp.repeat(counts, SLOTS, axis=1)).astype(jnp.bfloat16)
    groups = USERS // N_ROW

    def one_group(packed):
        index_rows, rating_rows, live_rows = packed
        chosen = jnp.take(item_factors, index_rows, axis=0)
        weighted = (chosen * live_rows[:, :, None]).astype(jnp.float32)
        scaled = (rating_rows * live_rows).astype(jnp.float32)
        normal_sum = jnp.einsum('usa,usb->uab', weighted, weighted, precision=lax.Precision.HIGHEST)
        right_side = jnp.einsum('us,usa->ua', scaled, weighted, precision=lax.Precision.HIGHEST)
        return (normal_sum, right_side)
    normal_sum, right_side = lax.map(one_group, (global_index.reshape(groups, N_ROW, -1), ratings.reshape(groups, N_ROW, -1), live_slot.reshape(groups, N_ROW, -1)))
    normal_sum = normal_sum.reshape(USERS, RANK, RANK)
    right_side = right_side.reshape(USERS, RANK)
    number = jnp.sum(counts.astype(jnp.float32), axis=1)
    answer = solve_users(normal_sum, right_side, number)
    return answer.reshape(N_COL, USERS // N_COL, RANK)
```

```python
import functools

import jax
import jax.numpy as jnp
from jax import lax
from jax.experimental import pallas as pl
from jax.experimental.pallas import tpu as pltpu
from jax.sharding import PartitionSpec as P

PANEL = 8
TILE = 256


def lane(x, i):
    where = jnp.full(x.shape, i, jnp.int32)
    return jnp.take_along_axis(x, where, axis=1, mode="promise_in_bounds")


def factor_and_solve(a_ref, l_ref, y, shift, users, rank):
    lanes = lax.broadcasted_iota(jnp.int32, (users, rank), 1)

    def slab(i):
        return pl.ds(pl.multiple_of(i * users, users), users)

    def panel(b, carry):
        y, inv_diag = carry
        i0 = b * PANEL
        rows = []
        for t in range(PANEL):
            rows.append(a_ref[slab(i0 + t), :] + jnp.where(lanes == i0 + t, shift, 0.0))
        right, low = [], []
        for t in range(PANEL):
            i = i0 + t
            inv = 1.0 / lane(rows[t], i)
            upper = jnp.where(lanes > i, rows[t], 0.0)
            scaled = upper * inv
            for t2 in range(t + 1, PANEL):
                rows[t2] = rows[t2] - lane(scaled, i0 + t2) * upper
            y = y - lane(y, i) * scaled
            inv_diag = jnp.where(lanes == i, inv, inv_diag)
            l_ref[slab(i), :] = jnp.where(lanes < i, rows[t], 0.0)
            right.append(upper)
            low.append(scaled)

        def trailing(g, _):
            for r in range(PANEL):
                j = g * PANEL + r
                acc = a_ref[slab(j), :]
                for t in range(PANEL):
                    acc = acc - lane(low[t], j) * right[t]
                a_ref[slab(j), :] = acc
            return 0

        lax.fori_loop(b + 1, rank // PANEL, trailing, 0)
        return y, inv_diag

    y, inv_diag = lax.fori_loop(0, rank // PANEL, panel, (y, jnp.zeros_like(y)))

    def back(b, x):
        for r in range(PANEL):
            j = rank - 1 - (b * PANEL + r)
            x = x - lane(x, j) * (l_ref[slab(j), :] * inv_diag)
        return x

    return lax.fori_loop(0, rank // PANEL, back, y * inv_diag)


def kernel(item_ref, slot_ref, out_ref, x_ref, a_ref, l_ref):
    n_block, items, rank = item_ref.shape
    users, slots = slot_ref.shape[1], slot_ref.shape[2] // 3
    halves = items // TILE
    pad = x_ref.shape[1] - rank
    entry = lax.broadcasted_iota(jnp.int32, (TILE, slots), 0).astype(jnp.float32)
    first = lax.broadcasted_iota(jnp.int32, (pad, slots), 0) == 0

    def block(k, number):
        table = item_ref[k].T
        left = jnp.concatenate([table[:, h * TILE : (h + 1) * TILE] for h in range(halves)], axis=0)
        packed = slot_ref[k].astype(jnp.float32)
        low, high, rate = packed[:, :slots], packed[:, slots : 2 * slots], packed[:, 2 * slots :]
        here = pl.ds(pl.multiple_of(k * slots, slots), slots)
        for u in range(users):
            hot = (entry == low[u : u + 1]).astype(jnp.bfloat16)
            picked = jnp.dot(left, hot, preferred_element_type=jnp.float32)
            rows = jnp.zeros((rank, slots), jnp.float32)
            for h in range(halves):
                rows = jnp.where(high[u : u + 1] == h, picked[h * rank : (h + 1) * rank], rows)
            x_ref[u, 0:rank, here] = rows.astype(jnp.bfloat16)
            x_ref[u, rank:, here] = jnp.where(first, rate[u : u + 1], 0.0).astype(jnp.bfloat16)
        return number + jnp.sum((high >= 0).astype(jnp.float32), axis=1, keepdims=True)

    number = lax.fori_loop(0, n_block, block, jnp.zeros((users, 1), jnp.float32))
    for u in range(users):
        full = lax.dot_general(
            x_ref[u], x_ref[u, 0:rank, :], (((1,), (1,)), ((), ())), preferred_element_type=jnp.float32
        )
        a_ref[pl.ds(u, rank + 8, stride=users), :] = full[: rank + 8]
    y = a_ref[rank * users : (rank + 1) * users, :]
    out_ref[...] = factor_and_solve(a_ref, l_ref, y, 0.1 * number / rank, users, rank)


def solve(items, slots_in, rank):
    n_block, users, width = slots_in.shape
    return pl.pallas_call(
        kernel,
        out_shape=jax.ShapeDtypeStruct((users, rank), jnp.float32),
        in_specs=[pl.BlockSpec(memory_space=pltpu.VMEM)] * 2,
        out_specs=pl.BlockSpec(memory_space=pltpu.VMEM),
        scratch_shapes=[
            pltpu.VMEM((users, rank + 16, n_block * width // 3), jnp.bfloat16),
            pltpu.VMEM(((rank + 8) * users, rank), jnp.float32),
            pltpu.VMEM((rank * users, rank), jnp.float32),
        ],
        compiler_params=pltpu.CompilerParams(vmem_limit_bytes=48 * 1024 * 1024),
    )(items, slots_in)


def per_device(n_row, item_factors, item_index, ratings, counts):
    rank = item_factors.shape[1]
    users, slots = item_index.shape
    items = lax.all_gather(item_factors, ("row", "col"), axis=0, tiled=True)
    items = items.reshape(n_row, -1, rank)
    live = lax.broadcasted_iota(jnp.int32, item_index.shape, 1) < counts
    low = (item_index % TILE).astype(jnp.bfloat16)
    high = jnp.where(live, item_index // TILE, -1).astype(jnp.bfloat16)
    packed = jnp.concatenate([low, high, ratings], axis=1).reshape(n_row, users // n_row, 3 * slots)
    moved = lax.all_to_all(packed, "row", split_axis=0, concat_axis=0, tiled=True)
    return solve(items, moved, rank)[None]


def solution(mesh):
    return jax.shard_map(
        functools.partial(per_device, mesh.shape["row"]),
        mesh=mesh,
        in_specs=(P(("row", "col"), None), P("col", "row"), P("col", "row"), P("col", "row")),
        out_specs=P("col", "row", None),
        check_vma=False,
    )
```

```python
import functools

import jax
import jax.numpy as jnp
from jax import lax
from jax.experimental import pallas as pl
from jax.experimental.pallas import tpu as pltpu
from jax.sharding import PartitionSpec as P

PANEL = 8
GROUP = 32
TILE = 256


def lane(x, i):
    where = jnp.full(x.shape, i, jnp.int32)
    return jnp.take_along_axis(x, where, axis=1, mode="promise_in_bounds")


def factor_and_solve(a_ref, l_ref, s_ref, y, shift, users, rank):
    lanes = lax.broadcasted_iota(jnp.int32, (users, rank), 1)

    def slab(i):
        return pl.ds(pl.multiple_of(i * users, users), users)

    def panel(first, last, b, carry):
        y, inv_diag = carry
        i0 = b * PANEL
        rows = []
        for t in range(PANEL):
            rows.append(a_ref[slab(i0 + t), :] + jnp.where(lanes == i0 + t, shift, 0.0))
        small = {(t, t2): lane(rows[t], i0 + t2) for t in range(PANEL) for t2 in range(t, PANEL)}
        side = [lane(y, i0 + t) for t in range(PANEL)]
        right, low = [], []
        for t in range(PANEL):
            i = i0 + t
            inv = 1.0 / small[t, t]
            for t2 in range(t + 1, PANEL):
                ratio = small[t, t2] * inv
                side[t2] = side[t2] - side[t] * ratio
                for t3 in range(t2, PANEL):
                    small[t2, t3] = small[t2, t3] - ratio * small[t, t3]
            upper = jnp.where(lanes > i, rows[t], 0.0)
            scaled = upper * inv
            for t2 in range(t + 1, PANEL):
                rows[t2] = rows[t2] - small[t, t2] * scaled
            y = y - side[t] * scaled
            inv_diag = jnp.where(lanes == i, inv, inv_diag)
            l_ref[slab(i), :] = jnp.where(lanes < i, rows[t], 0.0)
            s_ref[0, slab(i - first * PANEL), :] = scaled
            s_ref[1, slab(i - first * PANEL), :] = upper
            right.append(upper)
            low.append(scaled)

        def trailing(g, _):
            for r in range(PANEL):
                j = g * PANEL + r
                acc = a_ref[slab(j), :]
                for t in range(PANEL):
                    acc = acc - lane(low[t], j) * right[t]
                a_ref[slab(j), :] = acc
            return 0

        lax.fori_loop(b + 1, last, trailing, 0)
        return y, inv_diag

    carry = (y, jnp.zeros_like(y))
    step = GROUP // PANEL
    for q in range(rank // GROUP):
        carry = lax.fori_loop(q * step, (q + 1) * step, functools.partial(panel, q * step, (q + 1) * step), carry)
        done = (q + 1) * GROUP
        if done < rank:
            for u in range(users):
                mine = pl.ds(u, GROUP, stride=users)
                left = s_ref[0, mine, :].T[done:]
                update = jnp.dot(
                    left, s_ref[1, mine, :], precision=lax.Precision.HIGHEST, preferred_element_type=jnp.float32
                )
                rest = pl.ds(done * users + u, rank - done, stride=users)
                a_ref[rest, :] = a_ref[rest, :] - update
    y, inv_diag = carry

    def back(b, x):
        j0 = rank - 1 - b * PANEL
        rows = [l_ref[slab(j0 - r), :] * inv_diag for r in range(PANEL)]
        part = [lane(x, j0 - r) for r in range(PANEL)]
        for r in range(PANEL):
            for r2 in range(r + 1, PANEL):
                part[r2] = part[r2] - part[r] * lane(rows[r], j0 - r2)
            x = x - part[r] * rows[r]
        return x

    return lax.fori_loop(0, rank // PANEL, back, y * inv_diag)


def kernel(item_ref, slot_ref, out_ref, x_ref, a_ref, l_ref, s_ref):
    n_block, items, rank = item_ref.shape
    users, slots = slot_ref.shape[1], slot_ref.shape[2] // 3
    halves = items // TILE
    pad = x_ref.shape[1] - rank
    entry = lax.broadcasted_iota(jnp.int32, (TILE, slots), 0).astype(jnp.float32)
    first = lax.broadcasted_iota(jnp.int32, (pad, slots), 0) == 0

    def block(k, number):
        table = item_ref[k].T
        left = jnp.concatenate([table[:, h * TILE : (h + 1) * TILE] for h in range(halves)], axis=0)
        packed = slot_ref[k].astype(jnp.float32)
        low, high, rate = packed[:, :slots], packed[:, slots : 2 * slots], packed[:, 2 * slots :]
        here = pl.ds(pl.multiple_of(k * slots, slots), slots)
        for u in range(users):
            hot = (entry == low[u : u + 1]).astype(jnp.bfloat16)
            picked = jnp.dot(left, hot, preferred_element_type=jnp.float32)
            rows = jnp.zeros((rank, slots), jnp.float32)
            for h in range(halves):
                rows = jnp.where(high[u : u + 1] == h, picked[h * rank : (h + 1) * rank], rows)
            x_ref[u, 0:rank, here] = rows.astype(jnp.bfloat16)
            x_ref[u, rank:, here] = jnp.where(first, rate[u : u + 1], 0.0).astype(jnp.bfloat16)
        return number + jnp.sum((high >= 0).astype(jnp.float32), axis=1, keepdims=True)

    number = lax.fori_loop(0, n_block, block, jnp.zeros((users, 1), jnp.float32))
    for u in range(users):
        full = lax.dot_general(
            x_ref[u], x_ref[u, 0:rank, :], (((1,), (1,)), ((), ())), preferred_element_type=jnp.float32
        )
        a_ref[pl.ds(u, rank + 8, stride=users), :] = full[: rank + 8]
    y = a_ref[rank * users : (rank + 1) * users, :]
    out_ref[...] = factor_and_solve(a_ref, l_ref, s_ref, y, 0.1 * number / rank, users, rank)


def solve(items, slots_in, rank):
    n_block, users, width = slots_in.shape
    return pl.pallas_call(
        kernel,
        out_shape=jax.ShapeDtypeStruct((users, rank), jnp.float32),
        in_specs=[pl.BlockSpec(memory_space=pltpu.VMEM)] * 2,
        out_specs=pl.BlockSpec(memory_space=pltpu.VMEM),
        scratch_shapes=[
            pltpu.VMEM((users, rank + 16, n_block * width // 3), jnp.bfloat16),
            pltpu.VMEM(((rank + 8) * users, rank), jnp.float32),
            pltpu.VMEM((rank * users, rank), jnp.float32),
            pltpu.VMEM((2, GROUP * users, rank), jnp.float32),
        ],
        compiler_params=pltpu.CompilerParams(vmem_limit_bytes=48 * 1024 * 1024),
    )(items, slots_in)


def exchange_kernel(n_row, n_col, item_ref, slot_ref, all_ref, got_ref, own_sem, z_sem, far_sem, near_sem, slot_sem):
    row, col = lax.axis_index("row"), lax.axis_index("col")
    half = n_row // 2
    twin = row + 1 - 2 * lax.rem(row, 2)

    def col_at(d):
        return lax.rem(col + d, n_col)

    def row_at(d):
        return lax.rem(row + d, n_row)

    def far(d):
        return lax.rem(row + 2 * d, n_row)

    barrier = pltpu.get_barrier_semaphore()
    for d in range(1, n_col):
        pl.semaphore_signal(barrier, inc=1, device_id=(row, col_at(d)), device_id_type=pl.DeviceIdType.MESH)
    for d in range(1, n_row):
        pl.semaphore_signal(barrier, inc=1, device_id=(row_at(d), col), device_id_type=pl.DeviceIdType.MESH)

    own_items = pltpu.make_async_copy(item_ref, all_ref.at[row, col], own_sem.at[0])
    own_items.start()
    own_slots = pltpu.make_async_copy(slot_ref.at[row], got_ref.at[row], own_sem.at[1])
    own_slots.start()
    pl.semaphore_wait(barrier, n_col + n_row - 2)

    def send(src, dst, sems, where):
        copy = pltpu.make_async_remote_copy(
            src_ref=src,
            dst_ref=dst,
            send_sem=sems[0],
            recv_sem=sems[1],
            device_id=where,
            device_id_type=pl.DeviceIdType.MESH,
        )
        copy.start()
        return copy

    along = {}
    for d in range(1, n_col):
        sems = z_sem.at[0, d], z_sem.at[1, d]
        along[d] = send(item_ref, all_ref.at[row, col], sems, (row, col_at(d)))
    across, pair = {}, {}

    def spread(d, src):
        piece = lax.rem(col - d + n_col, n_col)
        for e in range(1, half):
            sems = far_sem.at[0, d, e], far_sem.at[1, d, e]
            across[d, e] = send(src, all_ref.at[row, piece], sems, (far(e), col))
        sems = near_sem.at[0, d, 0], near_sem.at[1, d, 0]
        pair[d, 0] = send(src, all_ref.at[row, piece], sems, (twin, col))

    spread(0, item_ref)
    slots = []
    for d in range(1, n_row):
        to = row_at(d)
        slots.append(send(slot_ref.at[to], got_ref.at[row], (slot_sem.at[0, d], slot_sem.at[1, d]), (to, col)))
    for d in range(1, n_col):
        along[d].wait_recv()
        spread(d, all_ref.at[row, lax.rem(col - d + n_col, n_col)])
    for d in range(n_col):
        piece = lax.rem(col - d + n_col, n_col)
        for e in range(1, half):
            across[d, e].wait_recv()
            source = lax.rem(row - 2 * e + n_row, n_row)
            sems = near_sem.at[0, d, e], near_sem.at[1, d, e]
            pair[d, e] = send(all_ref.at[source, piece], all_ref.at[source, piece], sems, (twin, col))
    for copy in slots:
        copy.wait()
    for copy in along.values():
        copy.wait_send()
    for copy in across.values():
        copy.wait_send()
    for copy in pair.values():
        copy.wait()
    own_items.wait()
    own_slots.wait()


def exchange(n_row, n_col, items, packed):
    half = n_row // 2
    vmem = pl.BlockSpec(memory_space=pltpu.VMEM)
    return pl.pallas_call(
        functools.partial(exchange_kernel, n_row, n_col),
        out_shape=(
            jax.ShapeDtypeStruct((n_row, n_col) + items.shape, items.dtype),
            jax.ShapeDtypeStruct(packed.shape, packed.dtype),
        ),
        in_specs=[vmem] * 2,
        out_specs=(vmem, vmem),
        scratch_shapes=[
            pltpu.SemaphoreType.DMA((2,)),
            pltpu.SemaphoreType.DMA((2, n_col)),
            pltpu.SemaphoreType.DMA((2, n_col, half)),
            pltpu.SemaphoreType.DMA((2, n_col, half)),
            pltpu.SemaphoreType.DMA((2, n_row)),
        ],
        compiler_params=pltpu.CompilerParams(
            collective_id=0, has_side_effects=True, vmem_limit_bytes=24 * 1024 * 1024
        ),
    )(items, packed)


def per_device(n_row, n_col, item_factors, item_index, ratings, counts):
    rank = item_factors.shape[1]
    users, slots = item_index.shape
    live = lax.broadcasted_iota(jnp.int32, item_index.shape, 1) < counts
    low = (item_index % TILE).astype(jnp.bfloat16)
    high = jnp.where(live, item_index // TILE, -1).astype(jnp.bfloat16)
    packed = jnp.concatenate([low, high, ratings], axis=1).reshape(n_row, users // n_row, 3 * slots)
    items, moved = exchange(n_row, n_col, item_factors, packed)
    return solve(items.reshape(n_row, -1, rank), moved, rank)[None]


def solution(mesh):
    return jax.shard_map(
        functools.partial(per_device, mesh.shape["row"], mesh.shape["col"]),
        mesh=mesh,
        in_specs=(P(("row", "col"), None), P("col", "row"), P("col", "row"), P("col", "row")),
        out_specs=P("col", "row", None),
        check_vma=False,
    )
```

```python
import functools

import jax
import jax.numpy as jnp
from jax import lax
from jax.experimental import pallas as pl
from jax.experimental.pallas import tpu as pltpu
from jax.sharding import PartitionSpec as P

PANEL = 8
GROUP = 16
TILE = 256


def lane(x, i):
    where = jnp.full(x.shape, i, jnp.int32)
    return jnp.take_along_axis(x, where, axis=1, mode="promise_in_bounds")


def factor_and_solve(a_ref, l_ref, s_ref, y, shift, users, rank):
    lanes = lax.broadcasted_iota(jnp.int32, (users, rank), 1)

    def slab(i):
        return pl.ds(pl.multiple_of(i * users, users), users)

    def panel(first, last, b, carry):
        y, inv_diag = carry
        i0 = b * PANEL
        rows = []
        for t in range(PANEL):
            rows.append(a_ref[slab(i0 + t), :] + jnp.where(lanes == i0 + t, shift, 0.0))
        small = {(t, t2): lane(rows[t], i0 + t2) for t in range(PANEL) for t2 in range(t, PANEL)}
        side = [lane(y, i0 + t) for t in range(PANEL)]
        right, low = [], []
        for t in range(PANEL):
            i = i0 + t
            inv = 1.0 / small[t, t]
            for t2 in range(t + 1, PANEL):
                ratio = small[t, t2] * inv
                side[t2] = side[t2] - side[t] * ratio
                for t3 in range(t2, PANEL):
                    small[t2, t3] = small[t2, t3] - ratio * small[t, t3]
            upper = jnp.where(lanes > i, rows[t], 0.0)
            scaled = upper * inv
            for t2 in range(t + 1, PANEL):
                rows[t2] = rows[t2] - small[t, t2] * scaled
            y = y - side[t] * scaled
            inv_diag = jnp.where(lanes == i, inv, inv_diag)
            l_ref[slab(i), :] = jnp.where(lanes < i, rows[t], 0.0)
            s_ref[0, slab(i - first * PANEL), :] = scaled
            s_ref[1, slab(i - first * PANEL), :] = upper
            right.append(upper)
            low.append(scaled)

        def trailing(g, _):
            for r in range(PANEL):
                j = g * PANEL + r
                acc = a_ref[slab(j), :]
                for t in range(PANEL):
                    acc = acc - lane(low[t], j) * right[t]
                a_ref[slab(j), :] = acc
            return 0

        lax.fori_loop(b + 1, last, trailing, 0)
        return y, inv_diag

    carry = (y, jnp.zeros_like(y))
    step = GROUP // PANEL
    for q in range(rank // GROUP):
        carry = lax.fori_loop(q * step, (q + 1) * step, functools.partial(panel, q * step, (q + 1) * step), carry)
        done = (q + 1) * GROUP
        if done < rank:
            for u in range(users):
                mine = pl.ds(u, GROUP, stride=users)
                left = s_ref[0, mine, :].T[done:]
                update = jnp.dot(
                    left, s_ref[1, mine, :], precision=lax.Precision.HIGHEST, preferred_element_type=jnp.float32
                )
                rest = pl.ds(done * users + u, rank - done, stride=users)
                a_ref[rest, :] = a_ref[rest, :] - update
    y, inv_diag = carry

    def back(b, x):
        j0 = rank - 1 - b * PANEL
        rows = [l_ref[slab(j0 - r), :] * inv_diag for r in range(PANEL)]
        part = [lane(x, j0 - r) for r in range(PANEL)]
        for r in range(PANEL):
            for r2 in range(r + 1, PANEL):
                part[r2] = part[r2] - part[r] * lane(rows[r], j0 - r2)
            x = x - part[r] * rows[r]
        return x

    return lax.fori_loop(0, rank // PANEL, back, y * inv_diag)


def solve_kernel(full_ref, number_ref, out_ref, a_ref, l_ref, s_ref):
    users, rank = out_ref.shape
    for u in range(users):
        a_ref[pl.ds(u, rank + 8, stride=users), :] = full_ref[u, : rank + 8]
    y = a_ref[rank * users : (rank + 1) * users, :]
    out_ref[...] = factor_and_solve(a_ref, l_ref, s_ref, y, 0.1 * number_ref[...] / rank, users, rank)


def solve(full, number):
    users, rank = number.shape
    return pl.pallas_call(
        solve_kernel,
        out_shape=jax.ShapeDtypeStruct((users, rank), jnp.float32),
        in_specs=[pl.BlockSpec(memory_space=pltpu.VMEM)] * 2,
        out_specs=pl.BlockSpec(memory_space=pltpu.VMEM),
        scratch_shapes=[
            pltpu.VMEM(((rank + 8) * users, rank), jnp.float32),
            pltpu.VMEM((rank * users, rank), jnp.float32),
            pltpu.VMEM((2, GROUP * users, rank), jnp.float32),
        ],
        compiler_params=pltpu.CompilerParams(vmem_limit_bytes=16 * 1024 * 1024),
    )(full, number)


def place_block(items_ref, slot_ref, x_ref, k, number):
    n_col, depth, rank = items_ref.shape[1:]
    users, slots = slot_ref.shape[1], slot_ref.shape[2] // 3
    halves = n_col * depth // TILE
    pad = x_ref.shape[1] - rank
    entry = lax.broadcasted_iota(jnp.int32, (TILE, slots), 0).astype(jnp.float32)
    first = lax.broadcasted_iota(jnp.int32, (pad, slots), 0) == 0
    table = items_ref[k].reshape(n_col * depth, rank).T
    left = jnp.concatenate([table[:, h * TILE : (h + 1) * TILE] for h in range(halves)], axis=0)
    packed = slot_ref[k].astype(jnp.float32)
    low, high, rate = packed[:, :slots], packed[:, slots : 2 * slots], packed[:, 2 * slots :]
    here = pl.ds(pl.multiple_of(k * slots, slots), slots)
    for u in range(users):
        hot = (entry == low[u : u + 1]).astype(jnp.bfloat16)
        picked = jnp.dot(left, hot, preferred_element_type=jnp.float32)
        rows = jnp.zeros((rank, slots), jnp.float32)
        for h in range(halves):
            rows = jnp.where(high[u : u + 1] == h, picked[h * rank : (h + 1) * rank], rows)
        x_ref[u, 0:rank, here] = rows.astype(jnp.bfloat16)
        x_ref[u, rank:, here] = jnp.where(first, rate[u : u + 1], 0.0).astype(jnp.bfloat16)
    return number + jnp.sum((high >= 0).astype(jnp.float32), axis=1, keepdims=True)


def gather_kernel(
    n_row, n_col, item_ref, slot_ref, full_ref, number_ref,
    all_ref, got_ref, x_ref, own_sem, z_sem, far_sem, near_sem, slot_sem,
):
    row, col = lax.axis_index("row"), lax.axis_index("col")
    half = n_row // 2
    twin = row + 1 - 2 * lax.rem(row, 2)

    def col_at(d):
        return lax.rem(col + d, n_col)

    def row_at(d):
        return lax.rem(row + d, n_row)

    def far(d):
        return lax.rem(row + 2 * d, n_row)

    barrier = pltpu.get_barrier_semaphore()
    for d in range(1, n_col):
        pl.semaphore_signal(barrier, inc=1, device_id=(row, col_at(d)), device_id_type=pl.DeviceIdType.MESH)
    for d in range(1, n_row):
        pl.semaphore_signal(barrier, inc=1, device_id=(row_at(d), col), device_id_type=pl.DeviceIdType.MESH)

    own_items = pltpu.make_async_copy(item_ref, all_ref.at[row, col], own_sem.at[0])
    own_items.start()
    own_slots = pltpu.make_async_copy(slot_ref.at[row], got_ref.at[row], own_sem.at[1])
    own_slots.start()
    pl.semaphore_wait(barrier, n_col + n_row - 2)

    def send(src, dst, sems, where):
        copy = pltpu.make_async_remote_copy(
            src_ref=src,
            dst_ref=dst,
            send_sem=sems[0],
            recv_sem=sems[1],
            device_id=where,
            device_id_type=pl.DeviceIdType.MESH,
        )
        copy.start()
        return copy

    along = {}
    for d in range(1, n_col):
        sems = z_sem.at[0, d], z_sem.at[1, d]
        along[d] = send(item_ref, all_ref.at[row, col], sems, (row, col_at(d)))
    across, pair = {}, {}

    def spread(d, src):
        piece = lax.rem(col - d + n_col, n_col)
        for e in range(1, half):
            sems = far_sem.at[0, d, e], far_sem.at[1, d, e]
            across[d, e] = send(src, all_ref.at[row, piece], sems, (far(e), col))
        sems = near_sem.at[0, d, 0], near_sem.at[1, d, 0]
        pair[d, 0] = send(src, all_ref.at[row, piece], sems, (twin, col))

    spread(0, item_ref)
    slots = []
    for d in range(1, n_row):
        to = row_at(d)
        slots.append(send(slot_ref.at[to], got_ref.at[row], (slot_sem.at[0, d], slot_sem.at[1, d]), (to, col)))
    for d in range(1, n_col):
        along[d].wait_recv()
        spread(d, all_ref.at[row, lax.rem(col - d + n_col, n_col)])
    own_items.wait()
    own_slots.wait()
    for copy in slots:
        copy.wait_recv()
    users, rank = number_ref.shape
    number = place_block(all_ref, got_ref, x_ref, row, jnp.zeros((users, 1), jnp.float32))

    def across_copy(d, e):
        piece = lax.rem(col - d + n_col, n_col)
        source = lax.rem(row - 2 * e + n_row, n_row)
        return pltpu.make_async_remote_copy(
            src_ref=all_ref.at[source, piece],
            dst_ref=all_ref.at[source, piece],
            send_sem=far_sem.at[0, d, e],
            recv_sem=far_sem.at[1, d, e],
            device_id=(far(e), col),
            device_id_type=pl.DeviceIdType.MESH,
        )

    def pair_copy(d, e, start):
        piece = lax.rem(col - d + n_col, n_col)
        source = lax.rem(start - 2 * e + n_row, n_row)
        return pltpu.make_async_remote_copy(
            src_ref=all_ref.at[source, piece],
            dst_ref=all_ref.at[source, piece],
            send_sem=near_sem.at[0, d, e],
            recv_sem=near_sem.at[1, d, e],
            device_id=(twin, col),
            device_id_type=pl.DeviceIdType.MESH,
        )

    def same_core(e, number):
        for d in range(n_col):
            across_copy(d, e).wait_recv()
            pair_copy(d, e, row).start()
        return place_block(all_ref, got_ref, x_ref, lax.rem(row - 2 * e + n_row, n_row), number)

    number = lax.fori_loop(1, half, same_core, number)

    def other_core(e, number):
        for d in range(n_col):
            pair_copy(d, e, twin).wait_recv()
        return place_block(all_ref, got_ref, x_ref, lax.rem(twin - 2 * e + n_row, n_row), number)

    number = lax.fori_loop(0, half, other_core, number)
    number_ref[...] = jnp.broadcast_to(number, (users, rank))

    for u in range(users):
        full_ref[u] = lax.dot_general(
            x_ref[u], x_ref[u, 0:rank, :], (((1,), (1,)), ((), ())), preferred_element_type=jnp.float32
        )

    for copy in slots:
        copy.wait_send()
    for copy in along.values():
        copy.wait_send()
    for copy in across.values():
        copy.wait_send()
    for d in range(n_col):
        for e in range(half):
            pair_copy(d, e, row).wait_send()


def gather(n_row, n_col, items, packed):
    half = n_row // 2
    users, slots, rank = packed.shape[1], packed.shape[2] // 3, items.shape[1]
    vmem = pl.BlockSpec(memory_space=pltpu.VMEM)
    return pl.pallas_call(
        functools.partial(gather_kernel, n_row, n_col),
        out_shape=(
            jax.ShapeDtypeStruct((users, rank + 16, rank), jnp.float32),
            jax.ShapeDtypeStruct((users, rank), jnp.float32),
        ),
        in_specs=[vmem] * 2,
        out_specs=(vmem, vmem),
        scratch_shapes=[
            pltpu.VMEM((n_row, n_col) + items.shape, items.dtype),
            pltpu.VMEM(packed.shape, packed.dtype),
            pltpu.VMEM((users, rank + 16, n_row * slots), jnp.bfloat16),
            pltpu.SemaphoreType.DMA((2,)),
            pltpu.SemaphoreType.DMA((2, n_col)),
            pltpu.SemaphoreType.DMA((2, n_col, half)),
            pltpu.SemaphoreType.DMA((2, n_col, half)),
            pltpu.SemaphoreType.DMA((2, n_row)),
        ],
        compiler_params=pltpu.CompilerParams(
            collective_id=0, has_side_effects=True, vmem_limit_bytes=48 * 1024 * 1024
        ),
    )(items, packed)


def per_device(n_row, n_col, item_factors, item_index, ratings, counts):
    users, slots = item_index.shape
    live = lax.broadcasted_iota(jnp.int32, item_index.shape, 1) < counts
    low = (item_index % TILE).astype(jnp.bfloat16)
    high = jnp.where(live, item_index // TILE, -1).astype(jnp.bfloat16)
    packed = jnp.concatenate([low, high, ratings], axis=1).reshape(n_row, users // n_row, 3 * slots)
    return solve(*gather(n_row, n_col, item_factors, packed))[None]


def solution(mesh):
    return jax.shard_map(
        functools.partial(per_device, mesh.shape["row"], mesh.shape["col"]),
        mesh=mesh,
        in_specs=(P(("row", "col"), None), P("col", "row"), P("col", "row"), P("col", "row")),
        out_specs=P("col", "row", None),
        check_vma=False,
    )
```

```python
import functools

import jax
import jax.numpy as jnp
from jax import lax
from jax.experimental import pallas as pl
from jax.experimental.pallas import tpu as pltpu
from jax.sharding import PartitionSpec as P

PANEL = 8
GROUP = 16
TILE = 256


def lane(x, i):
    where = jnp.full(x.shape, i, jnp.int32)
    return jnp.take_along_axis(x, where, axis=1, mode="promise_in_bounds")


def split(x):
    x0 = x.astype(jnp.bfloat16)
    rest = x - x0.astype(jnp.float32)
    x1 = rest.astype(jnp.bfloat16)
    return x0, x1, (rest - x1.astype(jnp.float32)).astype(jnp.bfloat16)


def factor_and_solve(a_ref, l_ref, s_ref, y, shift, users, rank):
    lanes = lax.broadcasted_iota(jnp.int32, (users, rank), 1)

    def slab(i):
        return pl.ds(pl.multiple_of(i * users, users), users)

    def panel(first, last, b, carry):
        y, inv_diag = carry
        i0 = b * PANEL
        rows = []
        for t in range(PANEL):
            rows.append(a_ref[slab(i0 + t), :] + jnp.where(lanes == i0 + t, shift, 0.0))
        small = {(t, t2): lane(rows[t], i0 + t2) for t in range(PANEL) for t2 in range(t, PANEL)}
        side = [lane(y, i0 + t) for t in range(PANEL)]
        right, low = [], []
        for t in range(PANEL):
            i = i0 + t
            inv = 1.0 / small[t, t]
            for t2 in range(t + 1, PANEL):
                ratio = small[t, t2] * inv
                side[t2] = side[t2] - side[t] * ratio
                for t3 in range(t2, PANEL):
                    small[t2, t3] = small[t2, t3] - ratio * small[t, t3]
            upper = jnp.where(lanes > i, rows[t], 0.0)
            scaled = upper * inv
            for t2 in range(t + 1, PANEL):
                rows[t2] = rows[t2] - small[t, t2] * scaled
            y = y - side[t] * scaled
            inv_diag = jnp.where(lanes == i, inv, inv_diag)
            l_ref[slab(i), :] = jnp.where(lanes < i, rows[t], 0.0)
            s_ref[0, slab(i - first * PANEL), :] = scaled
            s_ref[1, slab(i - first * PANEL), :] = upper
            right.append(upper)
            low.append(scaled)

        def trailing(g, _):
            for r in range(PANEL):
                j = g * PANEL + r
                acc = a_ref[slab(j), :]
                for t in range(PANEL):
                    acc = acc - lane(low[t], j) * right[t]
                a_ref[slab(j), :] = acc
            return 0

        lax.fori_loop(b + 1, last, trailing, 0)
        return y, inv_diag

    carry = (y, jnp.zeros_like(y))
    step = GROUP // PANEL
    for q in range(rank // GROUP):
        carry = lax.fori_loop(q * step, (q + 1) * step, functools.partial(panel, q * step, (q + 1) * step), carry)
        done = (q + 1) * GROUP
        if done < rank:
            for u in range(users):
                mine = pl.ds(u, GROUP, stride=users)
                l0, l1, l2 = split(s_ref[0, mine, :])
                r0, r1, r2 = split(s_ref[1, mine, :])
                left = jnp.concatenate([l0, l0, l1, l0, l2, l1], axis=0)
                right = jnp.concatenate([r0, r1, r0, r2, r0, r1], axis=0)
                update = jnp.dot(left.T[done:], right, preferred_element_type=jnp.float32)
                rest = pl.ds(done * users + u, rank - done, stride=users)
                a_ref[rest, :] = a_ref[rest, :] - update
    y, inv_diag = carry

    def back(b, x):
        j0 = rank - 1 - b * PANEL
        rows = [l_ref[slab(j0 - r), :] * inv_diag for r in range(PANEL)]
        part = [lane(x, j0 - r) for r in range(PANEL)]
        for r in range(PANEL):
            for r2 in range(r + 1, PANEL):
                part[r2] = part[r2] - part[r] * lane(rows[r], j0 - r2)
            x = x - part[r] * rows[r]
        return x

    return lax.fori_loop(0, rank // PANEL, back, y * inv_diag)


def solve_kernel(full_ref, number_ref, out_ref, a_ref, l_ref, s_ref):
    users, rank = out_ref.shape
    for u in range(users):
        a_ref[pl.ds(u, rank + 8, stride=users), :] = full_ref[u, : rank + 8]
    y = a_ref[rank * users : (rank + 1) * users, :]
    out_ref[...] = factor_and_solve(a_ref, l_ref, s_ref, y, 0.1 * number_ref[...] / rank, users, rank)


def solve(full, number):
    users, rank = number.shape
    return pl.pallas_call(
        solve_kernel,
        out_shape=jax.ShapeDtypeStruct((users, rank), jnp.float32),
        in_specs=[pl.BlockSpec(memory_space=pltpu.VMEM)] * 2,
        out_specs=pl.BlockSpec(memory_space=pltpu.VMEM),
        scratch_shapes=[
            pltpu.VMEM(((rank + 8) * users, rank), jnp.float32),
            pltpu.VMEM((rank * users, rank), jnp.float32),
            pltpu.VMEM((2, GROUP * users, rank), jnp.float32),
        ],
        compiler_params=pltpu.CompilerParams(vmem_limit_bytes=16 * 1024 * 1024),
    )(full, number)


def place_block(items_ref, slot_ref, x_ref, k, number):
    n_col, depth, rank = items_ref.shape[1:]
    users, slots = slot_ref.shape[1], slot_ref.shape[2] // 3
    halves = n_col * depth // TILE
    pad = x_ref.shape[1] - rank
    entry = lax.broadcasted_iota(jnp.int32, (TILE, slots), 0).astype(jnp.float32)
    first = lax.broadcasted_iota(jnp.int32, (pad, slots), 0) == 0
    table = items_ref[k].reshape(n_col * depth, rank).T
    left = jnp.concatenate([table[:, h * TILE : (h + 1) * TILE] for h in range(halves)], axis=0)
    packed = slot_ref[k].astype(jnp.float32)
    low, high, rate = packed[:, :slots], packed[:, slots : 2 * slots], packed[:, 2 * slots :]
    here = pl.ds(pl.multiple_of(k * slots, slots), slots)
    for u in range(users):
        hot = (entry == low[u : u + 1]).astype(jnp.bfloat16)
        picked = jnp.dot(left, hot, preferred_element_type=jnp.float32)
        rows = jnp.zeros((rank, slots), jnp.float32)
        for h in range(halves):
            rows = jnp.where(high[u : u + 1] == h, picked[h * rank : (h + 1) * rank], rows)
        x_ref[u, 0:rank, here] = rows.astype(jnp.bfloat16)
        x_ref[u, rank:, here] = jnp.where(first, rate[u : u + 1], 0.0).astype(jnp.bfloat16)
    return number + jnp.sum((high >= 0).astype(jnp.float32), axis=1, keepdims=True)


def gather_kernel(
    n_row, n_col, item_ref, index_ref, rate_ref, count_ref, full_ref, number_ref,
    slot_ref, all_ref, got_ref, x_ref, own_sem, z_sem, far_sem, near_sem, slot_sem,
):
    row, col = lax.axis_index("row"), lax.axis_index("col")
    half = n_row // 2
    twin = row + 1 - 2 * lax.rem(row, 2)

    def col_at(d):
        return lax.rem(col + d, n_col)

    def row_at(d):
        return lax.rem(row + d, n_row)

    def far(d):
        return lax.rem(row + 2 * d, n_row)

    barrier = pltpu.get_barrier_semaphore()
    for d in range(1, n_col):
        pl.semaphore_signal(barrier, inc=1, device_id=(row, col_at(d)), device_id_type=pl.DeviceIdType.MESH)
    for d in range(1, n_row):
        pl.semaphore_signal(barrier, inc=1, device_id=(row_at(d), col), device_id_type=pl.DeviceIdType.MESH)

    users, rank = number_ref.shape
    slots_each = index_ref.shape[1]
    live = lax.broadcasted_iota(jnp.int32, index_ref.shape, 1) < count_ref[...]
    low = lax.rem(index_ref[...], TILE).astype(jnp.float32)
    high = jnp.where(live, lax.div(index_ref[...], TILE), -1).astype(jnp.float32)
    rate = rate_ref[...].astype(jnp.float32)
    for r in range(n_row):
        for part, values in enumerate((low, high, rate)):
            mine = values[r * users : (r + 1) * users].astype(jnp.bfloat16)
            slot_ref[r, :, part * slots_each : (part + 1) * slots_each] = mine

    own_items = pltpu.make_async_copy(item_ref, all_ref.at[row, col], own_sem.at[0])
    own_items.start()
    own_slots = pltpu.make_async_copy(slot_ref.at[row], got_ref.at[row], own_sem.at[1])
    own_slots.start()
    pl.semaphore_wait(barrier, n_col + n_row - 2)

    def send(src, dst, sems, where):
        copy = pltpu.make_async_remote_copy(
            src_ref=src,
            dst_ref=dst,
            send_sem=sems[0],
            recv_sem=sems[1],
            device_id=where,
            device_id_type=pl.DeviceIdType.MESH,
        )
        copy.start()
        return copy

    along = {}
    for d in range(1, n_col):
        sems = z_sem.at[0, d], z_sem.at[1, d]
        along[d] = send(item_ref, all_ref.at[row, col], sems, (row, col_at(d)))
    across, pair = {}, {}

    def spread(d, src):
        piece = lax.rem(col - d + n_col, n_col)
        for e in range(1, half):
            sems = far_sem.at[0, d, e], far_sem.at[1, d, e]
            across[d, e] = send(src, all_ref.at[row, piece], sems, (far(e), col))
        sems = near_sem.at[0, d, 0], near_sem.at[1, d, 0]
        pair[d, 0] = send(src, all_ref.at[row, piece], sems, (twin, col))

    spread(0, item_ref)
    slots = []
    for d in range(1, n_row):
        to = row_at(d)
        slots.append(send(slot_ref.at[to], got_ref.at[row], (slot_sem.at[0, d], slot_sem.at[1, d]), (to, col)))
    for d in range(1, n_col):
        along[d].wait_recv()
        spread(d, all_ref.at[row, lax.rem(col - d + n_col, n_col)])
    own_items.wait()
    own_slots.wait()
    for copy in slots:
        copy.wait_recv()
    def across_copy(d, e):
        piece = lax.rem(col - d + n_col, n_col)
        source = lax.rem(row - 2 * e + n_row, n_row)
        return pltpu.make_async_remote_copy(
            src_ref=all_ref.at[source, piece],
            dst_ref=all_ref.at[source, piece],
            send_sem=far_sem.at[0, d, e],
            recv_sem=far_sem.at[1, d, e],
            device_id=(far(e), col),
            device_id_type=pl.DeviceIdType.MESH,
        )

    def pair_copy(d, e, start):
        piece = lax.rem(col - d + n_col, n_col)
        source = lax.rem(start - 2 * e + n_row, n_row)
        return pltpu.make_async_remote_copy(
            src_ref=all_ref.at[source, piece],
            dst_ref=all_ref.at[source, piece],
            send_sem=near_sem.at[0, d, e],
            recv_sem=near_sem.at[1, d, e],
            device_id=(twin, col),
            device_id_type=pl.DeviceIdType.MESH,
        )

    def forward(d):
        for e in range(1, half):
            across_copy(d, e).wait_recv()
            pair_copy(d, e, row).start()

    def place(start, e, number):
        return place_block(all_ref, got_ref, x_ref, lax.rem(start - 2 * e + n_row, n_row), number)

    def arrive(e):
        for d in range(n_col):
            pair_copy(d, e, twin).wait_recv()

    forward(0)
    number = place(row, 0, jnp.zeros((users, 1), jnp.float32))
    for d in range(1, n_col // 2):
        forward(d)
    arrive(0)
    number = place(twin, 0, number)
    for d in range(max(1, n_col // 2), n_col):
        forward(d)
    number = lax.fori_loop(1, half, functools.partial(place, row), number)

    def other_core(e, number):
        arrive(e)
        return place(twin, e, number)

    number = lax.fori_loop(1, half, other_core, number)
    number_ref[...] = jnp.broadcast_to(number, (users, rank))

    for u in range(users):
        full_ref[u] = lax.dot_general(
            x_ref[u], x_ref[u, 0:rank, :], (((1,), (1,)), ((), ())), preferred_element_type=jnp.float32
        )

    for copy in slots:
        copy.wait_send()
    for copy in along.values():
        copy.wait_send()
    for copy in across.values():
        copy.wait_send()
    for d in range(n_col):
        for e in range(half):
            pair_copy(d, e, row).wait_send()


def gather(n_row, n_col, items, index, ratings, counts):
    half = n_row // 2
    users, slots, rank = index.shape[0] // n_row, index.shape[1], items.shape[1]
    packed = pltpu.VMEM((n_row, users, 3 * slots), jnp.bfloat16)
    vmem = pl.BlockSpec(memory_space=pltpu.VMEM)
    return pl.pallas_call(
        functools.partial(gather_kernel, n_row, n_col),
        out_shape=(
            jax.ShapeDtypeStruct((users, rank + 16, rank), jnp.float32),
            jax.ShapeDtypeStruct((users, rank), jnp.float32),
        ),
        in_specs=[vmem] * 4,
        out_specs=(vmem, vmem),
        scratch_shapes=[
            packed,
            pltpu.VMEM((n_row, n_col) + items.shape, items.dtype),
            packed,
            pltpu.VMEM((users, rank + 16, n_row * slots), jnp.bfloat16),
            pltpu.SemaphoreType.DMA((2,)),
            pltpu.SemaphoreType.DMA((2, n_col)),
            pltpu.SemaphoreType.DMA((2, n_col, half)),
            pltpu.SemaphoreType.DMA((2, n_col, half)),
            pltpu.SemaphoreType.DMA((2, n_row)),
        ],
        compiler_params=pltpu.CompilerParams(
            collective_id=0, has_side_effects=True, vmem_limit_bytes=48 * 1024 * 1024
        ),
    )(items, index, ratings, counts)


def per_device(n_row, n_col, item_factors, item_index, ratings, counts):
    return solve(*gather(n_row, n_col, item_factors, item_index, ratings, counts))[None]


def solution(mesh):
    return jax.shard_map(
        functools.partial(per_device, mesh.shape["row"], mesh.shape["col"]),
        mesh=mesh,
        in_specs=(P(("row", "col"), None), P("col", "row"), P("col", "row"), P("col", "row")),
        out_specs=P("col", "row", None),
        check_vma=False,
    )
```

```python
import functools

import jax
import jax.numpy as jnp
from jax import lax
from jax.experimental import pallas as pl
from jax.experimental.pallas import tpu as pltpu
from jax.sharding import PartitionSpec as P

PANEL = 8
GROUP = 16
TILE = 256


def lane(x, i):
    where = jnp.full(x.shape, i, jnp.int32)
    return jnp.take_along_axis(x, where, axis=1, mode="promise_in_bounds")


def split(x):
    x0 = x.astype(jnp.bfloat16)
    rest = x - x0.astype(jnp.float32)
    x1 = rest.astype(jnp.bfloat16)
    return x0, x1, (rest - x1.astype(jnp.float32)).astype(jnp.bfloat16)


def factor_and_solve(a_ref, l_ref, s_ref, y, shift, users, rank):
    lanes = lax.broadcasted_iota(jnp.int32, (users, rank), 1)

    def slab(i):
        return pl.ds(pl.multiple_of(i * users, users), users)

    def panel(first, last, b, carry):
        y, inv_diag = carry
        i0 = b * PANEL
        rows = []
        for t in range(PANEL):
            rows.append(a_ref[slab(i0 + t), :] + jnp.where(lanes == i0 + t, shift, 0.0))
        small = {(t, t2): lane(rows[t], i0 + t2) for t in range(PANEL) for t2 in range(t, PANEL)}
        side = [lane(y, i0 + t) for t in range(PANEL)]
        right, low = [], []
        for t in range(PANEL):
            i = i0 + t
            inv = 1.0 / small[t, t]
            for t2 in range(t + 1, PANEL):
                ratio = small[t, t2] * inv
                side[t2] = side[t2] - side[t] * ratio
                for t3 in range(t2, PANEL):
                    small[t2, t3] = small[t2, t3] - ratio * small[t, t3]
            upper = jnp.where(lanes > i, rows[t], 0.0)
            scaled = upper * inv
            for t2 in range(t + 1, PANEL):
                rows[t2] = rows[t2] - small[t, t2] * scaled
            y = y - side[t] * scaled
            inv_diag = jnp.where(lanes == i, inv, inv_diag)
            l_ref[slab(i), :] = jnp.where(lanes < i, rows[t], 0.0)
            s_ref[0, slab(i - first * PANEL), :] = scaled
            s_ref[1, slab(i - first * PANEL), :] = upper
            right.append(upper)
            low.append(scaled)

        def trailing(g, _):
            for r in range(PANEL):
                j = g * PANEL + r
                acc = a_ref[slab(j), :]
                for t in range(PANEL):
                    acc = acc - lane(low[t], j) * right[t]
                a_ref[slab(j), :] = acc
            return 0

        lax.fori_loop(b + 1, last, trailing, 0)
        return y, inv_diag

    carry = (y, jnp.zeros_like(y))
    step = GROUP // PANEL
    for q in range(rank // GROUP):
        carry = lax.fori_loop(q * step, (q + 1) * step, functools.partial(panel, q * step, (q + 1) * step), carry)
        done = (q + 1) * GROUP
        if done < rank:
            for u in range(users):
                mine = pl.ds(u, GROUP, stride=users)
                l0, l1, l2 = split(s_ref[0, mine, :])
                r0, r1, r2 = split(s_ref[1, mine, :])
                left = jnp.concatenate([l0, l0, l1, l0, l2, l1], axis=0)
                right = jnp.concatenate([r0, r1, r0, r2, r0, r1], axis=0)
                update = jnp.dot(left.T[done:], right, preferred_element_type=jnp.float32)
                rest = pl.ds(done * users + u, rank - done, stride=users)
                a_ref[rest, :] = a_ref[rest, :] - update
    y, inv_diag = carry

    def back(b, x):
        j0 = rank - 1 - b * PANEL
        rows = [l_ref[slab(j0 - r), :] * inv_diag for r in range(PANEL)]
        part = [lane(x, j0 - r) for r in range(PANEL)]
        for r in range(PANEL):
            for r2 in range(r + 1, PANEL):
                part[r2] = part[r2] - part[r] * lane(rows[r], j0 - r2)
            x = x - part[r] * rows[r]
        return x

    return lax.fori_loop(0, rank // PANEL, back, y * inv_diag)


def solve_kernel(full_ref, number_ref, out_ref, a_ref, l_ref, s_ref):
    users, rank = out_ref.shape
    for u in range(users):
        a_ref[pl.ds(u, rank + 8, stride=users), :] = full_ref[u, : rank + 8]
    y = a_ref[rank * users : (rank + 1) * users, :]
    out_ref[...] = factor_and_solve(a_ref, l_ref, s_ref, y, 0.1 * number_ref[...] / rank, users, rank)


def solve(full, number):
    users, rank = number.shape
    return pl.pallas_call(
        solve_kernel,
        out_shape=jax.ShapeDtypeStruct((users, rank), jnp.float32),
        in_specs=[pl.BlockSpec(memory_space=pltpu.VMEM)] * 2,
        out_specs=pl.BlockSpec(memory_space=pltpu.VMEM),
        scratch_shapes=[
            pltpu.VMEM(((rank + 8) * users, rank), jnp.float32),
            pltpu.VMEM((rank * users, rank), jnp.float32),
            pltpu.VMEM((2, GROUP * users, rank), jnp.float32),
        ],
        compiler_params=pltpu.CompilerParams(vmem_limit_bytes=16 * 1024 * 1024),
    )(full, number)


def place_block(items_ref, slot_ref, x_ref, k, number):
    n_col, depth, rank = items_ref.shape[1:]
    users, slots = slot_ref.shape[1], slot_ref.shape[2] // 3
    halves = n_col * depth // TILE
    pad = x_ref.shape[1] - rank
    entry = lax.broadcasted_iota(jnp.int32, (TILE, slots), 0).astype(jnp.float32)
    first = lax.broadcasted_iota(jnp.int32, (pad, slots), 0) == 0
    table = items_ref[k].reshape(n_col * depth, rank).T
    left = jnp.concatenate([table[:, h * TILE : (h + 1) * TILE] for h in range(halves)], axis=0)
    packed = slot_ref[k].astype(jnp.float32)
    low, high, rate = packed[:, :slots], packed[:, slots : 2 * slots], packed[:, 2 * slots :]
    here = pl.ds(pl.multiple_of(k * slots, slots), slots)
    for u in range(users):
        hot = (entry == low[u : u + 1]).astype(jnp.bfloat16)
        picked = jnp.dot(left, hot, preferred_element_type=jnp.float32)
        rows = jnp.zeros((rank, slots), jnp.float32)
        for h in range(halves):
            rows = jnp.where(high[u : u + 1] == h, picked[h * rank : (h + 1) * rank], rows)
        x_ref[u, 0:rank, here] = rows.astype(jnp.bfloat16)
        x_ref[u, rank:, here] = jnp.where(first, rate[u : u + 1], 0.0).astype(jnp.bfloat16)
    return number + jnp.sum((high >= 0).astype(jnp.float32), axis=1, keepdims=True)


def gather_kernel(
    n_row, n_col, item_ref, index_in, rate_in, count_in, full_ref, number_ref,
    index_ref, rate_ref, count_ref, in_sem, slot_ref, all_ref, got_ref, x_ref, own_sem, z_sem, far_sem, near_sem, slot_sem,
):
    row, col = lax.axis_index("row"), lax.axis_index("col")
    half = n_row // 2
    twin = row + 1 - 2 * lax.rem(row, 2)

    def col_at(d):
        return lax.rem(col + d, n_col)

    def row_at(d):
        return lax.rem(row + d, n_row)

    def far(d):
        return lax.rem(row + 2 * d, n_row)

    barrier = pltpu.get_barrier_semaphore()
    for d in range(1, n_col):
        pl.semaphore_signal(barrier, inc=1, device_id=(row, col_at(d)), device_id_type=pl.DeviceIdType.MESH)
    for d in range(1, n_row):
        pl.semaphore_signal(barrier, inc=1, device_id=(row_at(d), col), device_id_type=pl.DeviceIdType.MESH)

    loads = []
    for n, (src, dst) in enumerate(((index_in, index_ref), (rate_in, rate_ref), (count_in, count_ref))):
        loads.append(pltpu.make_async_copy(src, dst, in_sem.at[n]))
        loads[-1].start()
    own_items = pltpu.make_async_copy(item_ref, all_ref.at[row, col], own_sem.at[0])
    own_items.start()
    pl.semaphore_wait(barrier, n_col + n_row - 2)

    def send(src, dst, sems, where):
        copy = pltpu.make_async_remote_copy(
            src_ref=src,
            dst_ref=dst,
            send_sem=sems[0],
            recv_sem=sems[1],
            device_id=where,
            device_id_type=pl.DeviceIdType.MESH,
        )
        copy.start()
        return copy

    along = {}
    for d in range(1, n_col):
        sems = z_sem.at[0, d], z_sem.at[1, d]
        along[d] = send(item_ref, all_ref.at[row, col], sems, (row, col_at(d)))
    across, pair = {}, {}

    def spread(d, src):
        piece = lax.rem(col - d + n_col, n_col)
        for e in range(1, half):
            sems = far_sem.at[0, d, e], far_sem.at[1, d, e]
            across[d, e] = send(src, all_ref.at[row, piece], sems, (far(e), col))
        sems = near_sem.at[0, d, 0], near_sem.at[1, d, 0]
        pair[d, 0] = send(src, all_ref.at[row, piece], sems, (twin, col))

    spread(0, item_ref)
    for copy in loads:
        copy.wait()
    users, rank = number_ref.shape
    slots_each = index_ref.shape[1]
    square = (index_ref.shape[0],) * 2
    same = lax.broadcasted_iota(jnp.int32, square, 0) == lax.broadcasted_iota(jnp.int32, square, 1)
    count = jnp.sum(jnp.where(same, count_ref[...].astype(jnp.float32), 0.0), axis=1, keepdims=True)
    live = lax.broadcasted_iota(jnp.int32, index_ref.shape, 1).astype(jnp.float32) < count
    low = lax.rem(index_ref[...], TILE).astype(jnp.float32)
    high = jnp.where(live, lax.div(index_ref[...], TILE), -1).astype(jnp.float32)
    rate = rate_ref[...].astype(jnp.float32)
    for r in range(n_row):
        for part, values in enumerate((low, high, rate)):
            mine = values[r * users : (r + 1) * users].astype(jnp.bfloat16)
            slot_ref[r, :, part * slots_each : (part + 1) * slots_each] = mine

    own_slots = pltpu.make_async_copy(slot_ref.at[row], got_ref.at[row], own_sem.at[1])
    own_slots.start()
    slots = []
    for d in range(1, n_row):
        to = row_at(d)
        slots.append(send(slot_ref.at[to], got_ref.at[row], (slot_sem.at[0, d], slot_sem.at[1, d]), (to, col)))
    for d in range(1, n_col):
        along[d].wait_recv()
        spread(d, all_ref.at[row, lax.rem(col - d + n_col, n_col)])
    own_items.wait()
    own_slots.wait()
    for copy in slots:
        copy.wait_recv()
    def across_copy(d, e):
        piece = lax.rem(col - d + n_col, n_col)
        source = lax.rem(row - 2 * e + n_row, n_row)
        return pltpu.make_async_remote_copy(
            src_ref=all_ref.at[source, piece],
            dst_ref=all_ref.at[source, piece],
            send_sem=far_sem.at[0, d, e],
            recv_sem=far_sem.at[1, d, e],
            device_id=(far(e), col),
            device_id_type=pl.DeviceIdType.MESH,
        )

    def pair_copy(d, e, start):
        piece = lax.rem(col - d + n_col, n_col)
        source = lax.rem(start - 2 * e + n_row, n_row)
        return pltpu.make_async_remote_copy(
            src_ref=all_ref.at[source, piece],
            dst_ref=all_ref.at[source, piece],
            send_sem=near_sem.at[0, d, e],
            recv_sem=near_sem.at[1, d, e],
            device_id=(twin, col),
            device_id_type=pl.DeviceIdType.MESH,
        )

    def forward(d):
        for e in range(1, half):
            across_copy(d, e).wait_recv()
            pair_copy(d, e, row).start()

    def place(start, e, number):
        return place_block(all_ref, got_ref, x_ref, lax.rem(start - 2 * e + n_row, n_row), number)

    def arrive(e):
        for d in range(n_col):
            pair_copy(d, e, twin).wait_recv()

    forward(0)
    number = place(row, 0, jnp.zeros((users, 1), jnp.float32))
    for d in range(1, n_col // 2):
        forward(d)
    arrive(0)
    number = place(twin, 0, number)
    for d in range(max(1, n_col // 2), n_col):
        forward(d)
    number = lax.fori_loop(1, half, functools.partial(place, row), number)

    def other_core(e, number):
        arrive(e)
        return place(twin, e, number)

    number = lax.fori_loop(1, half, other_core, number)
    number_ref[...] = jnp.broadcast_to(number, (users, rank))

    for u in range(users):
        full_ref[u] = lax.dot_general(
            x_ref[u], x_ref[u, 0:rank, :], (((1,), (1,)), ((), ())), preferred_element_type=jnp.float32
        )

    for copy in slots:
        copy.wait_send()
    for copy in along.values():
        copy.wait_send()
    for copy in across.values():
        copy.wait_send()
    for d in range(n_col):
        for e in range(half):
            pair_copy(d, e, row).wait_send()


def gather(n_row, n_col, items, index, ratings, counts):
    half = n_row // 2
    users, slots, rank = index.shape[0] // n_row, index.shape[1], items.shape[1]
    packed = pltpu.VMEM((n_row, users, 3 * slots), jnp.bfloat16)
    vmem = pl.BlockSpec(memory_space=pltpu.VMEM)
    return pl.pallas_call(
        functools.partial(gather_kernel, n_row, n_col),
        out_shape=(
            jax.ShapeDtypeStruct((users, rank + 16, rank), jnp.float32),
            jax.ShapeDtypeStruct((users, rank), jnp.float32),
        ),
        in_specs=[pl.BlockSpec(memory_space=pltpu.HBM)] * 4,
        out_specs=(vmem, vmem),
        scratch_shapes=[
            pltpu.VMEM(index.shape, index.dtype),
            pltpu.VMEM(ratings.shape, ratings.dtype),
            pltpu.VMEM((1, counts.shape[0]), counts.dtype),
            pltpu.SemaphoreType.DMA((3,)),
            packed,
            pltpu.VMEM((n_row, n_col) + items.shape, items.dtype),
            packed,
            pltpu.VMEM((users, rank + 16, n_row * slots), jnp.bfloat16),
            pltpu.SemaphoreType.DMA((2,)),
            pltpu.SemaphoreType.DMA((2, n_col)),
            pltpu.SemaphoreType.DMA((2, n_col, half)),
            pltpu.SemaphoreType.DMA((2, n_col, half)),
            pltpu.SemaphoreType.DMA((2, n_row)),
        ],
        compiler_params=pltpu.CompilerParams(
            collective_id=0, has_side_effects=True, vmem_limit_bytes=60 * 1024 * 1024
        ),
    )(items, index, ratings, counts.reshape(1, -1))


def per_device(n_row, n_col, item_factors, item_index, ratings, counts):
    return solve(*gather(n_row, n_col, item_factors, item_index, ratings, counts))[None]


def solution(mesh):
    return jax.shard_map(
        functools.partial(per_device, mesh.shape["row"], mesh.shape["col"]),
        mesh=mesh,
        in_specs=(P(("row", "col"), None), P("col", "row"), P("col", "row"), P("col", "row")),
        out_specs=P("col", "row", None),
        check_vma=False,
    )
```
